512 devices in a mesh: dp: 64 (over z_hi, y, core), tensor: 8 (over z_lo, x).
Axes of the slice: x: 4, y: 8, z: 8 (z_hi: 4, z_lo: 2; z = z_hi * 2 + z_lo), core: 2. Of those that a mesh axis runs over, the one named last changes fastest.
Arguments:
- tokens: bfloat16 [32768, 8192], P('dp', 'tensor'), may hold values from -6 to 6
- value_weight: bfloat16 [8192, 1024], P('tensor', 'dp'), may hold values from -0.0625 to 0.0625
- adapter_down_weights: bfloat16 [8, 8192, 64], P(None, 'tensor'), may hold values from -0.0625 to 0.0625
- adapter_up_weights: bfloat16 [8, 64, 1024], P(None, None, 'tensor'), may hold values from -0.75 to 0.75
- value_gradient: bfloat16 [32768, 1024], P(('dp', 'tensor')), may hold values from -12 to 12
- block_adapter_index: int32 [256, 1], replicated, may hold values from 0 to 7
- block_live_rows: int32 [256], replicated, may hold values from 1 to 128
Outputs:
- values_out: bfloat16 [32768, 1024], P(('dp', 'tensor'))
- input_gradient: bfloat16 [32768, 8192], P('dp', 'tensor')
- grad_a: float32 [8, 8192, 64], P(None, 'tensor')
- grad_b: float32 [8, 64, 1024], P(None, None, 'tensor')
The draws below stay inside these ranges and needn't reach their ends.
Inputs may be any that keep to these rules, and one draw needn't show every extreme that they name: `block_adapter_index`: every adapter names at least one block.
All inputs are finite; a program needn't handle non-finite values.
Results may differ from the reference program's by a relative error of at most 0.02.
Values may be sent and summed in bfloat16 or wider, within the bound.
No kernel may reach another device: no remote copies, remote signals or barrier semaphores. Data moves between devices by JAX's collectives and lax.ppermute only.
A program may use at most 64 MiB of HBM per device.

```python
import jax
import jax.numpy as jnp
from jax import lax

MODEL_WIDTH = 8192
VALUE_COLUMNS = 1024
ADAPTER_RANK = 64
ADAPTER_COUNT = 8
BLK = 128
TOKENS = 32768
NBLK = 256
N_TENSOR = 8


def draw_block_live_rows(key, part):
    first_key, second_key, third_key = jax.random.split(key, 3)
    filled = jax.random.randint(first_key, (NBLK,), 1, BLK + 1).astype(jnp.int32)
    first_spot = jax.random.randint(second_key, (), 0, NBLK).astype(jnp.int32)
    offset = jax.random.randint(third_key, (), 0, NBLK - 1).astype(jnp.int32)
    second_spot = (first_spot + 1 + offset) % NBLK
    filled = filled.at[first_spot].set(BLK)
    filled = filled.at[second_spot].set(1)
    return filled.astype(jnp.int32)


def level_of(key, shape, pieces, smallest, top_value):
    level, own = 1.0, jax.random.fold_in(key, 6)
    for dim, blocks in pieces:
        heights = jnp.exp(jax.random.uniform(jax.random.fold_in(own, dim), (blocks,), jnp.float32, smallest / len(pieces), top_value / len(pieces)))
        level = level * jnp.repeat(heights, shape[dim] // blocks).reshape([-1 if axis == dim else 1 for axis in range(len(shape))])
    return level


def different_ones(own_key, rows, count, top, lift):
    sequence = jax.random.permutation(jax.random.fold_in(own_key, 1), count)
    pull = sequence
    for power in range(3):
        pull = pull * pull // count
    pull = pull * lift // count
    tickets = jax.random.randint(jax.random.fold_in(own_key, 2), (rows, count), 0, 4096) + pull
    holders = jax.random.permutation(jax.random.fold_in(own_key, 3), rows)[jnp.arange(count) % rows]
    tickets = jnp.where(jnp.arange(rows)[:, None] == holders[None, :], 1 << 14, tickets)
    merit = tickets * count + jnp.arange(count)
    return lax.top_k(merit.astype(jnp.int32), top)[1].astype(jnp.int32)


def bell_draw(stream_key, extent, scale, most, cuts=(), held_as=jnp.bfloat16):
    entries = scale * jax.random.normal(stream_key, extent, jnp.float32)
    if cuts:
        entries = entries * level_of(stream_key, extent, cuts, -0.22, 0.18)
    return jnp.clip(entries, -most, most).astype(held_as)


def setup_inputs(seed: int = 0) -> dict:
    key_list = jax.random.split(jax.random.key(seed), 8)
    tokens = bell_draw(key_list[0], (TOKENS, MODEL_WIDTH), 1.0, 6.0, ((0, 64), (1, 8)))
    value_weight = bell_draw(key_list[1], (MODEL_WIDTH, VALUE_COLUMNS), MODEL_WIDTH ** -0.5, 0.0625, ((0, 8), (1, 64)))
    adapter_down_weights = bell_draw(key_list[2], (ADAPTER_COUNT, MODEL_WIDTH, ADAPTER_RANK), MODEL_WIDTH ** -0.5, 0.0625, ((1, 8),))
    adapter_up_weights = bell_draw(key_list[3], (ADAPTER_COUNT, ADAPTER_RANK, VALUE_COLUMNS), ADAPTER_RANK ** -0.5, 0.75, ((2, 8),))
    value_gradient = bell_draw(key_list[4], (TOKENS, VALUE_COLUMNS), 2.0, 12.0, ((0, 512),))
    block_adapter_index = different_ones(key_list[5], NBLK, ADAPTER_COUNT, 1, 1024)
    block_live_rows = draw_block_live_rows(jax.random.fold_in(key_list[7], 71), 0)
    return {"tokens": tokens, "value_weight": value_weight, "adapter_down_weights": adapter_down_weights, "adapter_up_weights": adapter_up_weights, "value_gradient": value_gradient, "block_adapter_index": block_adapter_index, "block_live_rows": block_live_rows}


ADAPTER_SCALE = 2.0


def reference(tokens, value_weight, adapter_down_weights, adapter_up_weights, value_gradient, block_adapter_index, block_live_rows):
    width = MODEL_WIDTH // N_TENSOR
    blocks = TOKENS // BLK
    block_indices = block_adapter_index[:, 0]
    weight_parts = value_weight.reshape(N_TENSOR, width, VALUE_COLUMNS).astype(jnp.float32)
    token_block_rows = tokens.reshape(blocks, BLK, MODEL_WIDTH)
    grad_blocks = value_gradient.reshape(blocks, BLK, VALUE_COLUMNS)
    position = jnp.arange(BLK, dtype=jnp.int32)

    def advance(carry, item):
        total_a, total_b = carry
        rows_in, grads_in, identity_matrix, filled = item
        split_rows = rows_in.reshape(BLK, N_TENSOR, width).astype(jnp.float32)
        partials = jnp.einsum("knw,nwc->nkc", split_rows, weight_parts)
        partials = lax.optimization_barrier(partials.astype(jnp.bfloat16)).astype(jnp.float32)
        base = jnp.sum(partials, axis=0)
        down_matrix = adapter_down_weights[identity_matrix]
        up_matrix = adapter_up_weights[identity_matrix]
        reduced = jnp.dot(rows_in, down_matrix, preferred_element_type=jnp.float32).astype(jnp.bfloat16)
        values_blk = (base + ADAPTER_SCALE * jnp.dot(reduced, up_matrix, preferred_element_type=jnp.float32)).astype(jnp.bfloat16)
        live_mask = position < filled
        masked = jnp.where(live_mask[:, None], grads_in, jnp.zeros_like(grads_in))
        grad_low = jnp.dot(masked, up_matrix.T, preferred_element_type=jnp.float32).astype(jnp.bfloat16)
        back = jnp.dot(masked, value_weight.T, preferred_element_type=jnp.float32)
        back = back + ADAPTER_SCALE * jnp.dot(grad_low, down_matrix.T, preferred_element_type=jnp.float32)
        total_a = total_a.at[identity_matrix].add(jnp.dot(rows_in.T, grad_low, preferred_element_type=jnp.float32))
        total_b = total_b.at[identity_matrix].add(jnp.dot(reduced.T, masked, preferred_element_type=jnp.float32))
        return (total_a, total_b), (values_blk, back.astype(jnp.bfloat16))

    start = (jnp.zeros((ADAPTER_COUNT, MODEL_WIDTH, ADAPTER_RANK), jnp.float32), jnp.zeros((ADAPTER_COUNT, ADAPTER_RANK, VALUE_COLUMNS), jnp.float32))
    (total_a, total_b), (values_all, back_all) = lax.scan(advance, start, (token_block_rows, grad_blocks, block_indices, block_live_rows))
    onehot = (block_indices[:, None] == jnp.arange(ADAPTER_COUNT, dtype=jnp.int32)[None, :]).astype(jnp.float32)
    tallies = jnp.sum(onehot * block_live_rows[:, None].astype(jnp.float32), axis=0)
    factor = ADAPTER_SCALE / tallies
    return (values_all.reshape(TOKENS, VALUE_COLUMNS), back_all.reshape(TOKENS, MODEL_WIDTH),
            total_a * factor[:, None, None], total_b * factor[:, None, None])
```

```python
import jax
import jax.numpy as jnp
from jax import lax
from jax.experimental import pallas as pl
from jax.experimental.pallas import tpu as pltpu
from jax.sharding import PartitionSpec as P

BLK = 128
ADAPTER_SCALE = 2.0
F32 = jnp.float32
BF16 = jnp.bfloat16

TENSOR = 8
PEERS = 32
ROWS = 512
OWN = 64
BLOCKS = 4
WIDTH = 1024
COLS = 1024
HEAD = 128
RANK = 64
ADAPTERS = 8
TERM = WIDTH + HEAD
SEND_UP = 512
SEND_RED = 768
SEND = 1024

SMEM = pl.BlockSpec(memory_space=pltpu.SMEM)
VMEM = pl.BlockSpec(memory_space=pltpu.VMEM)
NT = (((1,), (1,)), ((), ()))
TN = (((0,), (0,)), ((), ()))


def call(kernel, ins, outs, flops, scratch=(), vmem=32):
    moved = sum(x.size * x.dtype.itemsize for x in (*ins, *outs))
    many = len(outs) > 1
    return pl.pallas_call(
        kernel,
        out_shape=tuple(outs) if many else outs[0],
        in_specs=[SMEM if x.dtype == jnp.int32 and x.ndim == 1 else VMEM for x in ins],
        out_specs=(VMEM,) * len(outs) if many else VMEM,
        scratch_shapes=list(scratch),
        compiler_params=pltpu.CompilerParams(vmem_limit_bytes=vmem * 1024 * 1024),
        cost_estimate=pl.CostEstimate(flops=flops, bytes_accessed=moved, transcendentals=0),
    )(*ins)


def out(shape, dtype=BF16):
    return jax.ShapeDtypeStruct(shape, dtype)


def dot(a, b, dims=(((1,), (0,)), ((), ()))):
    return lax.dot_general(a, b, dims, preferred_element_type=F32)


def pack_kernel(idx, live, pos, grad, up, tokens, down, send):
    data, tensor = pos[0], pos[1]
    block = tensor // 2
    row = (tensor % 2) * OWN + lax.broadcasted_iota(jnp.int32, (OWN, 128), 0)
    keep = row < live[data * BLOCKS + block]
    for k in range(COLS // 128):
        part = grad[:, k * 128 : (k + 1) * 128]
        part = jnp.where(keep, part.astype(F32), 0.0).astype(BF16)
        for p in range(TENSOR):
            send[p, k * OWN : (k + 1) * OWN, :] = part
    for b in range(BLOCKS):
        a = idx[data * BLOCKS + b]
        rows = up[a]
        red = dot(down[a], tokens[b * BLK : (b + 1) * BLK, :], NT).astype(BF16)
        for p in range(TENSOR):
            send[p, SEND_UP + b * RANK : SEND_UP + (b + 1) * RANK, :] = rows
            send[p, SEND_RED + b * RANK : SEND_RED + (b + 1) * RANK, :] = red


def terms_kernel(pos, got, tokens, masked, low, mine, theirs, update, red, ups, terms, block_update):
    data, tensor = pos[0], pos[1]
    core = data % 2
    for p in range(TENSOR):
        for k in range(COLS // 128):
            masked[p * OWN : (p + 1) * OWN, k * 128 : (k + 1) * 128] = got[p, k * OWN : (k + 1) * OWN, :]
        ups[:, p * HEAD : (p + 1) * HEAD] = got[p, SEND_UP:SEND_RED, :]
    total = got[0, SEND_RED:SEND, :].astype(F32)
    for p in range(1, TENSOR):
        total += got[p, SEND_RED:SEND, :].astype(F32)
    red[...] = total.astype(BF16)
    column = pl.multiple_of(tensor * OWN, OWN)
    for b in range(BLOCKS):
        rank = slice(b * RANK, (b + 1) * RANK)
        rows = slice(b * BLK, (b + 1) * BLK)
        projected = dot(ups[rank, :], masked[rows, :], NT).astype(BF16)
        low[rank, :] = projected
        terms[rank, :WIDTH] = dot(projected, tokens[rows, :]).astype(BF16)
        own = jnp.concatenate([got[2 * b, pl.ds(column, OWN), :], got[2 * b + 1, pl.ds(column, OWN), :]], axis=0)
        terms[rank, WIDTH:] = dot(red[rank, :], own).astype(BF16)
    for b in range(BLOCKS):
        here = pl.multiple_of(b * RANK + core * 32, 32)
        there = pl.multiple_of(b * RANK + (1 - core) * 32, 32)
        mine[b * 32 : (b + 1) * 32, :] = terms[pl.ds(here, 32), :]
        theirs[b * 32 : (b + 1) * 32, :] = terms[pl.ds(there, 32), :]
    first = pl.multiple_of((tensor // 2) * RANK, RANK)
    block_update[...] = ADAPTER_SCALE * dot(red[pl.ds(first, RANK), :], ups[pl.ds(first, RANK), :], TN)
    update[...] = block_update[pl.ds(pl.multiple_of((tensor % 2) * OWN, OWN), OWN), :]


def scatter_kernel(idx, pos, mine, theirs, by_peer):
    data = pos[0]
    row = lax.broadcasted_iota(jnp.int32, (PEERS * ADAPTERS, 128), 0)
    column = lax.broadcasted_iota(jnp.int32, (PEERS * ADAPTERS, 128), 1)

    def chosen(owner):
        block = column // 32
        adapter = jnp.where(
            block < 2,
            jnp.where(block == 0, idx[owner * BLOCKS], idx[owner * BLOCKS + 1]),
            jnp.where(block == 2, idx[owner * BLOCKS + 2], idx[owner * BLOCKS + 3]),
        )
        hit = (column % 32 == row // ADAPTERS) & (adapter == row % ADAPTERS)
        return jnp.where(hit, 1.0, 0.0).astype(BF16)

    sibling = data + 1 - 2 * (data % 2)
    by_peer[...] = (dot(chosen(data), mine[...]) + dot(chosen(sibling), theirs[...])).astype(BF16)


def total_kernel(idx, live, parts, spread):
    total = parts[0:16, :].astype(F32)
    for p in range(1, PEERS // 2):
        total += parts[p * 16 : (p + 1) * 16, :].astype(F32)
    total = total[:8, :] + total[8:, :]
    row = lax.broadcasted_iota(jnp.int32, (ADAPTERS, 128), 0)
    factor = jnp.zeros((ADAPTERS, 128), F32)
    for e in range(ADAPTERS):
        count = jnp.sum(jnp.where(idx[...] == e, live[...], 0).astype(F32), keepdims=True)
        factor = jnp.where(row == e, ADAPTER_SCALE / jnp.broadcast_to(count, (ADAPTERS, 128)), factor)
    for k in range(TERM // 128):
        lanes = slice(k * 128, (k + 1) * 128)
        scaled = total[:, lanes] * factor
        both = jnp.concatenate([scaled, scaled], axis=0).astype(BF16)
        for p in range(PEERS // 2):
            spread[p * 16 : (p + 1) * 16, lanes] = both


def unpack_kernel(pos, mine, theirs, grad_a, grad_b):
    core = pos[0] % 2
    row = lax.broadcasted_iota(jnp.int32, (256, 256), 0)
    column = lax.broadcasted_iota(jnp.int32, (256, 256), 1)
    order = jnp.where(column == (row % PEERS) * ADAPTERS + row // PEERS, 1.0, 0.0).astype(BF16)
    for half, rows in ((core, mine), (1 - core, theirs)):
        first = pl.multiple_of(half * PEERS, PEERS)
        for k in range(TERM // 128):
            lanes = slice(k * 128, (k + 1) * 128)
            part = dot(order, rows[:, lanes])
            for e in range(ADAPTERS):
                piece = part[e * PEERS : (e + 1) * PEERS, :]
                if k < WIDTH // 128:
                    grad_a[e, pl.ds(first, PEERS), lanes] = piece
                else:
                    grad_b[e, pl.ds(first, PEERS), :] = piece


def base_kernel(tokens, weight, base):
    for b in range(BLOCKS):
        rows = slice(b * BLK, (b + 1) * BLK)
        base[rows, :] = dot(tokens[rows, :], weight[...], NT).astype(BF16)


def input_kernel(idx, pos, masked, weight, low, down, grad):
    data = pos[0]
    for b in range(BLOCKS):
        rows = slice(b * BLK, (b + 1) * BLK)
        adapter = dot(low[b * RANK : (b + 1) * RANK, :], down[idx[data * BLOCKS + b]], TN)
        grad[rows, :] = (dot(masked[rows, :], weight[...]) + ADAPTER_SCALE * adapter).astype(BF16)


def shards(tokens, value_weight, down, up, value_gradient, block_adapter_index, block_live_rows):
    same_core = [list(range(core, 2 * PEERS, 2)) for core in range(2)]
    sibling = [(i, i ^ 1) for i in range(2 * PEERS)]
    pos = jnp.stack([lax.axis_index("dp"), lax.axis_index("tensor")]).astype(jnp.int32)
    idx = block_adapter_index[:, 0]
    live = block_live_rows
    down_t = jnp.swapaxes(down, 1, 2)
    weight = jnp.swapaxes(lax.all_gather(value_weight, "dp", axis=1, tiled=True), 0, 1)

    send = call(
        pack_kernel, (idx, live, pos, value_gradient, up, tokens, down_t),
        (out((TENSOR, SEND, 128)),), 2 * ROWS * WIDTH * RANK,
    )
    got = lax.all_to_all(send, "tensor", 0, 0, tiled=True)
    masked, low, mine, theirs, update = call(
        terms_kernel, (pos, got, tokens),
        (out((ROWS, COLS)), out((BLOCKS * RANK, BLK)), out((128, TERM)), out((128, TERM)), out((OWN, COLS), F32)),
        6 * ROWS * WIDTH * RANK,
        (
            pltpu.VMEM((BLOCKS * RANK, BLK), BF16),
            pltpu.VMEM((BLOCKS * RANK, COLS), BF16),
            pltpu.VMEM((BLOCKS * RANK, TERM), BF16),
            pltpu.VMEM((BLK, COLS), F32),
        ),
    )
    theirs = lax.ppermute(theirs, "dp", sibling)
    by_peer = call(scatter_kernel, (idx, pos, mine, theirs), (out((PEERS * ADAPTERS, TERM)),), 2 * 256 * 256 * TERM)
    parts = lax.all_to_all(by_peer, "dp", 0, 0, tiled=True, axis_index_groups=same_core)
    spread = call(
        total_kernel, (idx.reshape(2, 128), live.reshape(2, 128), parts),
        (out((PEERS * ADAPTERS, TERM)),), 256 * TERM,
    )
    half = lax.all_to_all(spread, "dp", 0, 0, tiled=True, axis_index_groups=same_core)
    other = lax.ppermute(half, "dp", sibling)
    grad_a, grad_b = call(
        unpack_kernel, (pos, half, other),
        (out((ADAPTERS, RANK, WIDTH), F32), out((ADAPTERS, RANK, HEAD), F32)), 4 * 256 * 256 * TERM,
    )

    base = call(base_kernel, (tokens, weight), (out((ROWS, COLS)),), 2 * ROWS * WIDTH * COLS)
    base_parts = lax.all_to_all(base, "tensor", 0, 0, tiled=True).reshape(TENSOR, OWN, COLS)
    input_gradient = call(
        input_kernel, (idx, pos, masked, weight, low, down_t), (out((ROWS, WIDTH)),),
        2 * ROWS * WIDTH * (COLS + RANK),
    )
    values_out = (jnp.sum(base_parts.astype(F32), axis=0) + update).astype(BF16)
    return values_out, input_gradient, jnp.swapaxes(grad_a, 1, 2), grad_b


def solution(mesh):
    return jax.shard_map(
        shards,
        mesh=mesh,
        in_specs=(
            P("dp", "tensor"),
            P("tensor", "dp"),
            P(None, "tensor", None),
            P(None, None, "tensor"),
            P(("dp", "tensor"), None),
            P(),
            P(),
        ),
        out_specs=(
            P(("dp", "tensor"), None),
            P("dp", "tensor"),
            P(None, "tensor", None),
            P(None, None, "tensor"),
        ),
        check_vma=False,
    )
```

```python
import jax
import jax.numpy as jnp
from jax import lax
from jax.experimental import pallas as pl
from jax.experimental.pallas import tpu as pltpu
from jax.sharding import Mesh
from jax.sharding import PartitionSpec as P

BLK = 128
ADAPTER_SCALE = 2.0
F32 = jnp.float32
BF16 = jnp.bfloat16

TENSOR = 8
PEERS = 32
ROWS = 512
OWN = 64
BLOCKS = 4
WIDTH = 1024
COLS = 1024
HEAD = 128
RANK = 64
ADAPTERS = 8
TERM = WIDTH + HEAD
Z_HI = 4
STRIPE = 16
PLANE = COLS // Z_HI
AXES = {"z_hi": Z_HI, "y": 8, "core": 2, "z_lo": 2, "x": 4}
DP = ("z_hi", "y", "core")
PEER = ("z_hi", "y")
TP = ("z_lo", "x")
SEND_UP = 512
SEND_RED = 768
SEND = 1024

SMEM = pl.BlockSpec(memory_space=pltpu.SMEM)
ANY = pl.BlockSpec(memory_space=pl.ANY)
VMEM = pl.BlockSpec(memory_space=pltpu.VMEM)
NT = (((1,), (1,)), ((), ()))
TN = (((0,), (0,)), ((), ()))


def call(kernel, ins, outs, flops, scratch=(), vmem=32, in_place=()):
    moved = sum(x.size * x.dtype.itemsize for x in (*ins, *outs))
    many = len(outs) > 1
    return pl.pallas_call(
        kernel,
        out_shape=tuple(outs) if many else outs[0],
        in_specs=[
            SMEM if x.dtype == jnp.int32 and x.ndim == 1 else ANY if i in in_place else VMEM
            for i, x in enumerate(ins)
        ],
        out_specs=(VMEM,) * len(outs) if many else VMEM,
        scratch_shapes=list(scratch),
        compiler_params=pltpu.CompilerParams(vmem_limit_bytes=vmem * 1024 * 1024),
        cost_estimate=pl.CostEstimate(flops=flops, bytes_accessed=moved, transcendentals=0),
    )(*ins)


def out(shape, dtype=BF16):
    return jax.ShapeDtypeStruct(shape, dtype)


def dot(a, b, dims=(((1,), (0,)), ((), ()))):
    return lax.dot_general(a, b, dims, preferred_element_type=F32)


def after(value, earlier):
    return pl.pallas_call(
        lambda value_in, earlier_in, value_out: None,
        out_shape=out(value.shape, value.dtype),
        in_specs=[ANY, ANY],
        out_specs=ANY,
        input_output_aliases={0: 0},
        cost_estimate=pl.CostEstimate(flops=0, bytes_accessed=0, transcendentals=0),
    )(value, earlier)


def pack_kernel(idx, live, pos, grad_in, up_in, tokens_in, down_in, send, grad, up, tokens, down, sems):
    data, tensor = pos[0], pos[1]
    copies = []
    for b in range(BLOCKS):
        a = idx[data * BLOCKS + b]
        rows = pl.ds(b * BLK, BLK)
        copies.append(
            (
                pltpu.make_async_copy(down_in.at[a], down.at[b], sems.at[b]),
                pltpu.make_async_copy(tokens_in.at[rows], tokens.at[rows], sems.at[BLOCKS + b]),
                pltpu.make_async_copy(up_in.at[a], up.at[b], sems.at[2 * BLOCKS + b]),
            )
        )
    grad_copy = pltpu.make_async_copy(grad_in, grad, sems.at[3 * BLOCKS])
    grad_copy.start()
    for group in copies:
        for copy in group:
            copy.start()
    block = tensor // 2
    row = (tensor % 2) * OWN + lax.broadcasted_iota(jnp.int32, (OWN, 128), 0)
    keep = row < live[data * BLOCKS + block]
    grad_copy.wait()
    for k in range(COLS // 128):
        part = grad[:, k * 128 : (k + 1) * 128]
        part = jnp.where(keep, part.astype(F32), 0.0).astype(BF16)
        for p in range(TENSOR):
            send[p, k * OWN : (k + 1) * OWN, :] = part
    for b in range(BLOCKS):
        for copy in copies[b]:
            copy.wait()
        rows = up[b]
        red = dot(down[b], tokens[b * BLK : (b + 1) * BLK, :], NT).astype(BF16)
        for p in range(TENSOR):
            send[p, SEND_UP + b * RANK : SEND_UP + (b + 1) * RANK, :] = rows
            send[p, SEND_RED + b * RANK : SEND_RED + (b + 1) * RANK, :] = red


def unpack_rows(got, masked):
    for p in range(TENSOR):
        for k in range(COLS // 128):
            masked[p * OWN : (p + 1) * OWN, k * 128 : (k + 1) * 128] = got[p, k * OWN : (k + 1) * OWN, :]


def terms_kernel(pos, got, tokens, low, mine, theirs, update, masked, red, ups, terms, block_update):
    data, tensor = pos[0], pos[1]
    core = data % 2
    for p in range(TENSOR):
        ups[:, p * HEAD : (p + 1) * HEAD] = got[p, SEND_UP:SEND_RED, :]
    unpack_rows(got, masked)
    total = got[0, SEND_RED:SEND, :].astype(F32)
    for p in range(1, TENSOR):
        total += got[p, SEND_RED:SEND, :].astype(F32)
    red[...] = total.astype(BF16)
    column = pl.multiple_of(tensor * OWN, OWN)
    for b in range(BLOCKS):
        rank = slice(b * RANK, (b + 1) * RANK)
        rows = slice(b * BLK, (b + 1) * BLK)
        projected = dot(ups[rank, :], masked[rows, :], NT).astype(BF16)
        low[rank, :] = projected
        terms[rank, :WIDTH] = dot(projected, tokens[rows, :]).astype(BF16)
        own = jnp.concatenate([got[2 * b, pl.ds(column, OWN), :], got[2 * b + 1, pl.ds(column, OWN), :]], axis=0)
        terms[rank, WIDTH:] = dot(red[rank, :], own).astype(BF16)
    for b in range(BLOCKS):
        here = pl.multiple_of(b * RANK + core * 32, 32)
        there = pl.multiple_of(b * RANK + (1 - core) * 32, 32)
        mine[b * 32 : (b + 1) * 32, :] = terms[pl.ds(here, 32), :]
        theirs[b * 32 : (b + 1) * 32, :] = terms[pl.ds(there, 32), :]
    first = pl.multiple_of((tensor // 2) * RANK, RANK)
    block_update[...] = ADAPTER_SCALE * dot(red[pl.ds(first, RANK), :], ups[pl.ds(first, RANK), :], TN)
    update[...] = block_update[pl.ds(pl.multiple_of((tensor % 2) * OWN, OWN), OWN), :]


def scatter_kernel(idx, pos, mine, theirs, by_peer):
    data = pos[0]
    row = lax.broadcasted_iota(jnp.int32, (PEERS * ADAPTERS, 128), 0)
    column = lax.broadcasted_iota(jnp.int32, (PEERS * ADAPTERS, 128), 1)

    def chosen(owner):
        block = column // 32
        adapter = jnp.where(
            block < 2,
            jnp.where(block == 0, idx[owner * BLOCKS], idx[owner * BLOCKS + 1]),
            jnp.where(block == 2, idx[owner * BLOCKS + 2], idx[owner * BLOCKS + 3]),
        )
        hit = (column % 32 == row // ADAPTERS) & (adapter == row % ADAPTERS)
        return jnp.where(hit, 1.0, 0.0).astype(BF16)

    sibling = data + 1 - 2 * (data % 2)
    by_peer[...] = (dot(chosen(data), mine[...]) + dot(chosen(sibling), theirs[...])).astype(BF16)


def total_kernel(idx, live, parts, spread):
    total = parts[0:16, :].astype(F32)
    for p in range(1, PEERS // 2):
        total += parts[p * 16 : (p + 1) * 16, :].astype(F32)
    total = total[:8, :] + total[8:, :]
    row = lax.broadcasted_iota(jnp.int32, (ADAPTERS, 128), 0)
    factor = jnp.zeros((ADAPTERS, 128), F32)
    for e in range(ADAPTERS):
        count = jnp.sum(jnp.where(idx[...] == e, live[...], 0).astype(F32), keepdims=True)
        factor = jnp.where(row == e, ADAPTER_SCALE / jnp.broadcast_to(count, (ADAPTERS, 128)), factor)
    for k in range(TERM // 128):
        lanes = slice(k * 128, (k + 1) * 128)
        scaled = total[:, lanes] * factor
        both = jnp.concatenate([scaled, scaled], axis=0).astype(BF16)
        for p in range(PEERS // 2):
            spread[p * 16 : (p + 1) * 16, lanes] = both


def unpack_kernel(pos, mine, theirs, grad_a, grad_b):
    core = pos[0] % 2
    row = lax.broadcasted_iota(jnp.int32, (256, 256), 0)
    column = lax.broadcasted_iota(jnp.int32, (256, 256), 1)
    order = jnp.where(column == (row % PEERS) * ADAPTERS + row // PEERS, 1.0, 0.0).astype(BF16)
    for half, rows in ((core, mine), (1 - core, theirs)):
        first = pl.multiple_of(half * PEERS, PEERS)
        for k in range(TERM // 128):
            lanes = slice(k * 128, (k + 1) * 128)
            part = dot(order, rows[:, lanes])
            for e in range(ADAPTERS):
                piece = part[e * PEERS : (e + 1) * PEERS, :]
                if k < WIDTH // 128:
                    grad_a[e, pl.ds(first, PEERS), lanes] = piece
                else:
                    grad_b[e, pl.ds(first, PEERS), :] = piece


def base_kernel(tokens, weight, base):
    for k in range(Z_HI):
        columns = slice(k * PLANE, (k + 1) * PLANE)
        base[:, columns] = dot(tokens[...], weight[columns, :], NT).astype(BF16)


def input_kernel(idx, pos, got, weight, low, down, grad, masked):
    data = pos[0]
    unpack_rows(got, masked)
    for b in range(BLOCKS):
        rows = slice(b * BLK, (b + 1) * BLK)
        adapter = dot(low[b * RANK : (b + 1) * RANK, :], down[idx[data * BLOCKS + b]], TN)
        grad[rows, :] = (dot(masked[rows, :], weight[...]) + ADAPTER_SCALE * adapter).astype(BF16)


def shards(tokens, value_weight, down, up, value_gradient, block_adapter_index, block_live_rows):
    sibling = [(0, 1), (1, 0)]
    pos = jnp.stack([lax.axis_index(DP), lax.axis_index(TP)]).astype(jnp.int32)
    idx = block_adapter_index[:, 0]
    live = block_live_rows
    down_t = jnp.swapaxes(down, 1, 2)

    stripes = jnp.broadcast_to(jnp.swapaxes(value_weight, 0, 1), (Z_HI, STRIPE, WIDTH))
    stripes = lax.all_to_all(stripes, "z_hi", 0, 0, tiled=True)
    send = call(
        pack_kernel, (idx, live, pos, value_gradient, up, tokens, down_t),
        (out((TENSOR, SEND, 128)),), 2 * ROWS * WIDTH * RANK,
        (
            pltpu.VMEM((OWN, COLS), BF16),
            pltpu.VMEM((BLOCKS, RANK, HEAD), BF16),
            pltpu.VMEM((ROWS, WIDTH), BF16),
            pltpu.VMEM((BLOCKS, RANK, WIDTH), BF16),
            pltpu.SemaphoreType.DMA((3 * BLOCKS + 1,)),
        ),
        vmem=56, in_place=range(3, 8),
    )
    send = after(send, stripes)
    weight = lax.all_gather(stripes, ("y", "core"), axis=1, tiled=False).reshape(COLS, WIDTH)
    got = lax.all_to_all(send, TP, 0, 0, tiled=True)
    low, mine, theirs, update = call(
        terms_kernel, (pos, got, tokens),
        (out((BLOCKS * RANK, BLK)), out((128, TERM)), out((128, TERM)), out((OWN, COLS), F32)),
        6 * ROWS * WIDTH * RANK,
        (
            pltpu.VMEM((ROWS, COLS), BF16),
            pltpu.VMEM((BLOCKS * RANK, BLK), BF16),
            pltpu.VMEM((BLOCKS * RANK, COLS), BF16),
            pltpu.VMEM((BLOCKS * RANK, TERM), BF16),
            pltpu.VMEM((BLK, COLS), F32),
        ),
    )
    theirs = lax.ppermute(theirs, "core", sibling)
    by_peer = call(scatter_kernel, (idx, pos, mine, theirs), (out((PEERS * ADAPTERS, TERM)),), 2 * 256 * 256 * TERM)
    parts = lax.all_to_all(by_peer, PEER, 0, 0, tiled=True)
    base = call(base_kernel, (tokens, weight), (out((ROWS, COLS)),), 2 * ROWS * WIDTH * COLS)
    own_base = lax.psum_scatter(base, TP, scatter_dimension=0, tiled=True)
    parts, _ = lax.optimization_barrier((parts, base))
    spread = call(
        total_kernel, (idx.reshape(2, 128), live.reshape(2, 128), parts),
        (out((PEERS * ADAPTERS, TERM)),), 256 * TERM,
    )
    half = lax.all_to_all(spread, PEER, 0, 0, tiled=True)
    input_gradient = call(
        input_kernel, (idx, pos, got, weight, low, down_t), (out((ROWS, WIDTH)),),
        2 * ROWS * WIDTH * (COLS + RANK), (pltpu.VMEM((ROWS, COLS), BF16),),
    )
    half, input_gradient = lax.optimization_barrier((half, input_gradient))
    other = lax.ppermute(half, "core", sibling)
    grad_a, grad_b = call(
        unpack_kernel, (pos, half, other),
        (out((ADAPTERS, RANK, WIDTH), F32), out((ADAPTERS, RANK, HEAD), F32)), 4 * 256 * 256 * TERM,
    )
    own_base, grad_b = lax.optimization_barrier((own_base, grad_b))
    values_out = (own_base.astype(F32) + update).astype(BF16)
    return values_out, input_gradient, jnp.swapaxes(grad_a, 1, 2), grad_b


def solution(mesh):
    grid = Mesh(mesh.devices.reshape(tuple(AXES.values())), tuple(AXES))
    return jax.shard_map(
        shards,
        mesh=grid,
        in_specs=(
            P(DP, TP),
            P(TP, DP),
            P(None, TP, None),
            P(None, None, TP),
            P((*DP, *TP), None),
            P(),
            P(),
        ),
        out_specs=(
            P((*DP, *TP), None),
            P(DP, TP),
            P(None, TP, None),
            P(None, None, TP),
        ),
        check_vma=False,
    )
```

```python
import jax
import jax.numpy as jnp
from jax import lax
from jax.experimental import pallas as pl
from jax.experimental.pallas import tpu as pltpu
from jax.sharding import Mesh
from jax.sharding import PartitionSpec as P

BLK = 128
ADAPTER_SCALE = 2.0
F32 = jnp.float32
BF16 = jnp.bfloat16

TENSOR = 8
PEERS = 32
ROWS = 512
OWN = 64
BLOCKS = 4
WIDTH = 1024
COLS = 1024
HEAD = 128
RANK = 64
ADAPTERS = 8
TERM = WIDTH + HEAD
Z_HI = 4
STRIPE = 16
PLANE = COLS // Z_HI
AXES = {"z_hi": Z_HI, "y": 8, "core": 2, "z_lo": 2, "x": 4}
DP = ("z_hi", "y", "core")
PEER = ("z_hi", "y")
TP = ("z_lo", "x")
SEND_UP = 512
SEND_RED = 768
SEND = 1024

SMEM = pl.BlockSpec(memory_space=pltpu.SMEM)
ANY = pl.BlockSpec(memory_space=pl.ANY)
VMEM = pl.BlockSpec(memory_space=pltpu.VMEM)
NT = (((1,), (1,)), ((), ()))
TN = (((0,), (0,)), ((), ()))


def call(kernel, ins, outs, flops, scratch=(), vmem=32, in_place=()):
    moved = sum(x.size * x.dtype.itemsize for x in (*ins, *outs))
    many = len(outs) > 1
    return pl.pallas_call(
        kernel,
        out_shape=tuple(outs) if many else outs[0],
        in_specs=[
            SMEM if x.dtype == jnp.int32 and x.ndim == 1 else ANY if i in in_place else VMEM
            for i, x in enumerate(ins)
        ],
        out_specs=(VMEM,) * len(outs) if many else VMEM,
        scratch_shapes=list(scratch),
        compiler_params=pltpu.CompilerParams(vmem_limit_bytes=vmem * 1024 * 1024),
        cost_estimate=pl.CostEstimate(flops=flops, bytes_accessed=moved, transcendentals=0),
    )(*ins)


def out(shape, dtype=BF16):
    return jax.ShapeDtypeStruct(shape, dtype)


def dot(a, b, dims=(((1,), (0,)), ((), ()))):
    return lax.dot_general(a, b, dims, preferred_element_type=F32)


def pack_kernel(idx, live, grad_in, up_in, tokens_in, down_in, send, grad, up, tokens, down, sems):
    data, tensor = lax.axis_index(DP), lax.axis_index(TP)
    copies = []
    for b in range(BLOCKS):
        a = idx[data * BLOCKS + b]
        rows = pl.ds(b * BLK, BLK)
        copies.append(
            (
                pltpu.make_async_copy(down_in.at[a], down.at[b], sems.at[b]),
                pltpu.make_async_copy(tokens_in.at[rows], tokens.at[rows], sems.at[BLOCKS + b]),
                pltpu.make_async_copy(up_in.at[a], up.at[b], sems.at[2 * BLOCKS + b]),
            )
        )
    grad_copy = pltpu.make_async_copy(grad_in, grad, sems.at[3 * BLOCKS])
    grad_copy.start()
    for group in copies:
        for copy in group:
            copy.start()
    block = tensor // 2
    row = (tensor % 2) * OWN + lax.broadcasted_iota(jnp.int32, (OWN, 128), 0)
    keep = row < live[data * BLOCKS + block]
    grad_copy.wait()
    for k in range(COLS // 128):
        part = grad[:, k * 128 : (k + 1) * 128]
        part = jnp.where(keep, part.astype(F32), 0.0).astype(BF16)
        for p in range(TENSOR):
            send[p, k * OWN : (k + 1) * OWN, :] = part
    for b in range(BLOCKS):
        for copy in copies[b]:
            copy.wait()
        rows = up[b]
        red = dot(down[b], tokens[b * BLK : (b + 1) * BLK, :], NT).astype(BF16)
        for p in range(TENSOR):
            send[p, SEND_UP + b * RANK : SEND_UP + (b + 1) * RANK, :] = rows
            send[p, SEND_RED + b * RANK : SEND_RED + (b + 1) * RANK, :] = red


def unpack_rows(got, masked):
    for p in range(TENSOR):
        for k in range(COLS // 128):
            masked[p * OWN : (p + 1) * OWN, k * 128 : (k + 1) * 128] = got[p, k * OWN : (k + 1) * OWN, :]


def terms_kernel(got, tokens, low, mine, theirs, update, masked, red, ups, terms, block_update):
    data, tensor = lax.axis_index(DP), lax.axis_index(TP)
    core = data % 2
    for p in range(TENSOR):
        ups[:, p * HEAD : (p + 1) * HEAD] = got[p, SEND_UP:SEND_RED, :]
    unpack_rows(got, masked)
    total = got[0, SEND_RED:SEND, :].astype(F32)
    for p in range(1, TENSOR):
        total += got[p, SEND_RED:SEND, :].astype(F32)
    red[...] = total.astype(BF16)
    column = pl.multiple_of(tensor * OWN, OWN)
    for b in range(BLOCKS):
        rank = slice(b * RANK, (b + 1) * RANK)
        rows = slice(b * BLK, (b + 1) * BLK)
        projected = dot(ups[rank, :], masked[rows, :], NT).astype(BF16)
        low[rank, :] = projected
        terms[rank, :WIDTH] = dot(projected, tokens[rows, :]).astype(BF16)
        own = jnp.concatenate([got[2 * b, pl.ds(column, OWN), :], got[2 * b + 1, pl.ds(column, OWN), :]], axis=0)
        terms[rank, WIDTH:] = dot(red[rank, :], own).astype(BF16)
    for b in range(BLOCKS):
        here = pl.multiple_of(b * RANK + core * 32, 32)
        there = pl.multiple_of(b * RANK + (1 - core) * 32, 32)
        mine[b * 32 : (b + 1) * 32, :] = terms[pl.ds(here, 32), :]
        theirs[b * 32 : (b + 1) * 32, :] = terms[pl.ds(there, 32), :]
    first = pl.multiple_of((tensor // 2) * RANK, RANK)
    block_update[...] = ADAPTER_SCALE * dot(red[pl.ds(first, RANK), :], ups[pl.ds(first, RANK), :], TN)
    update[...] = block_update[pl.ds(pl.multiple_of((tensor % 2) * OWN, OWN), OWN), :]


def scatter_kernel(idx, mine, theirs, by_peer):
    data = lax.axis_index(DP)
    row = lax.broadcasted_iota(jnp.int32, (PEERS * ADAPTERS, 128), 0)
    column = lax.broadcasted_iota(jnp.int32, (PEERS * ADAPTERS, 128), 1)

    def chosen(owner):
        block = column // 32
        adapter = jnp.where(
            block < 2,
            jnp.where(block == 0, idx[owner * BLOCKS], idx[owner * BLOCKS + 1]),
            jnp.where(block == 2, idx[owner * BLOCKS + 2], idx[owner * BLOCKS + 3]),
        )
        hit = (column % 32 == row // ADAPTERS) & (adapter == row % ADAPTERS)
        return jnp.where(hit, 1.0, 0.0).astype(BF16)

    sibling = data + 1 - 2 * (data % 2)
    by_peer[...] = (dot(chosen(data), mine[...]) + dot(chosen(sibling), theirs[...])).astype(BF16)


def total_kernel(idx, live, parts, spread):
    total = parts[0:16, :].astype(F32)
    for p in range(1, PEERS // 2):
        total += parts[p * 16 : (p + 1) * 16, :].astype(F32)
    total = total[:8, :] + total[8:, :]
    row = lax.broadcasted_iota(jnp.int32, (ADAPTERS, 128), 0)
    factor = jnp.zeros((ADAPTERS, 128), F32)
    for e in range(ADAPTERS):
        count = jnp.sum(jnp.where(idx[...] == e, live[...], 0).astype(F32), keepdims=True)
        factor = jnp.where(row == e, ADAPTER_SCALE / jnp.broadcast_to(count, (ADAPTERS, 128)), factor)
    for k in range(TERM // 128):
        lanes = slice(k * 128, (k + 1) * 128)
        scaled = total[:, lanes] * factor
        both = jnp.concatenate([scaled, scaled], axis=0).astype(BF16)
        for p in range(PEERS // 2):
            spread[p * 16 : (p + 1) * 16, lanes] = both


def unpack_kernel(mine, theirs, grad_a, grad_b):
    core = lax.axis_index(DP) % 2
    row = lax.broadcasted_iota(jnp.int32, (256, 256), 0)
    column = lax.broadcasted_iota(jnp.int32, (256, 256), 1)
    order = jnp.where(column == (row % PEERS) * ADAPTERS + row // PEERS, 1.0, 0.0).astype(BF16)
    for half, rows in ((core, mine), (1 - core, theirs)):
        first = pl.multiple_of(half * PEERS, PEERS)
        for k in range(TERM // 128):
            lanes = slice(k * 128, (k + 1) * 128)
            part = dot(order, rows[:, lanes])
            for e in range(ADAPTERS):
                piece = part[e * PEERS : (e + 1) * PEERS, :]
                if k < WIDTH // 128:
                    grad_a[e, pl.ds(first, PEERS), lanes] = piece
                else:
                    grad_b[e, pl.ds(first, PEERS), :] = piece


def base_kernel(tokens, weight, base):
    for k in range(Z_HI):
        columns = slice(k * PLANE, (k + 1) * PLANE)
        base[:, columns] = dot(tokens[...], weight[columns, :], NT).astype(BF16)


def input_kernel(idx, got, weight, low, down, grad, masked):
    data = lax.axis_index(DP)
    unpack_rows(got, masked)
    for b in range(BLOCKS):
        rows = slice(b * BLK, (b + 1) * BLK)
        adapter = dot(low[b * RANK : (b + 1) * RANK, :], down[idx[data * BLOCKS + b]], TN)
        grad[rows, :] = (dot(masked[rows, :], weight[...]) + ADAPTER_SCALE * adapter).astype(BF16)


def shards(tokens, value_weight, down, up, value_gradient, block_adapter_index, block_live_rows):
    sibling = [(0, 1), (1, 0)]
    idx = block_adapter_index[:, 0]
    live = block_live_rows
    down_t = jnp.swapaxes(down, 1, 2)

    stripes = jnp.broadcast_to(jnp.swapaxes(value_weight, 0, 1), (Z_HI, STRIPE, WIDTH))
    stripes = lax.all_to_all(stripes, "z_hi", 0, 0, tiled=True)
    send = call(
        pack_kernel, (idx, live, value_gradient, up, tokens, down_t),
        (out((TENSOR, SEND, 128)),), 2 * ROWS * WIDTH * RANK,
        (
            pltpu.VMEM((OWN, COLS), BF16),
            pltpu.VMEM((BLOCKS, RANK, HEAD), BF16),
            pltpu.VMEM((ROWS, WIDTH), BF16),
            pltpu.VMEM((BLOCKS, RANK, WIDTH), BF16),
            pltpu.SemaphoreType.DMA((3 * BLOCKS + 1,)),
        ),
        vmem=56, in_place=range(2, 6),
    )
    weight = lax.all_gather(stripes, ("y", "core"), axis=1, tiled=False).reshape(COLS, WIDTH)
    got = lax.all_to_all(send, TP, 0, 0, tiled=True)
    low, mine, theirs, update = call(
        terms_kernel, (got, tokens),
        (out((BLOCKS * RANK, BLK)), out((128, TERM)), out((128, TERM)), out((OWN, COLS), F32)),
        6 * ROWS * WIDTH * RANK,
        (
            pltpu.VMEM((ROWS, COLS), BF16),
            pltpu.VMEM((BLOCKS * RANK, BLK), BF16),
            pltpu.VMEM((BLOCKS * RANK, COLS), BF16),
            pltpu.VMEM((BLOCKS * RANK, TERM), BF16),
            pltpu.VMEM((BLK, COLS), F32),
        ),
    )
    theirs = lax.ppermute(theirs, "core", sibling)
    by_peer = call(scatter_kernel, (idx, mine, theirs), (out((PEERS * ADAPTERS, TERM)),), 2 * 256 * 256 * TERM)
    parts = lax.all_to_all(by_peer, PEER, 0, 0, tiled=True)
    base = call(base_kernel, (tokens, weight), (out((ROWS, COLS)),), 2 * ROWS * WIDTH * COLS)
    own_base = lax.psum_scatter(base, TP, scatter_dimension=0, tiled=True)
    parts, _ = lax.optimization_barrier((parts, base))
    spread = call(
        total_kernel, (idx.reshape(2, 128), live.reshape(2, 128), parts),
        (out((PEERS * ADAPTERS, TERM)),), 256 * TERM,
    )
    half = lax.all_to_all(spread, PEER, 0, 0, tiled=True)
    input_gradient = call(
        input_kernel, (idx, got, weight, low, down_t), (out((ROWS, WIDTH)),),
        2 * ROWS * WIDTH * (COLS + RANK), (pltpu.VMEM((ROWS, COLS), BF16),),
    )
    half, input_gradient = lax.optimization_barrier((half, input_gradient))
    other = lax.ppermute(half, "core", sibling)
    grad_a, grad_b = call(
        unpack_kernel, (half, other),
        (out((ADAPTERS, RANK, WIDTH), F32), out((ADAPTERS, RANK, HEAD), F32)), 4 * 256 * 256 * TERM,
    )
    own_base, grad_b = lax.optimization_barrier((own_base, grad_b))
    values_out = (own_base.astype(F32) + update).astype(BF16)
    return values_out, input_gradient, jnp.swapaxes(grad_a, 1, 2), grad_b


def solution(mesh):
    grid = Mesh(mesh.devices.reshape(tuple(AXES.values())), tuple(AXES))
    return jax.shard_map(
        shards,
        mesh=grid,
        in_specs=(
            P(DP, TP),
            P(TP, DP),
            P(None, TP, None),
            P(None, None, TP),
            P((*DP, *TP), None),
            P(),
            P(),
        ),
        out_specs=(
            P((*DP, *TP), None),
            P(DP, TP),
            P(None, TP, None),
            P(None, None, TP),
        ),
        check_vma=False,
    )
```
